32 devices in a mesh: seq: 8 (over z, x), dp: 4 (over y, core).
Axes of the slice: x: 2, y: 2, z: 4, core: 2. Of those that a mesh axis runs over, the one named last changes fastest.
Arguments:
- tokens: bfloat16 [8, 4096, 768], P('dp', 'seq'), may hold values from -6 to 6
- starts: int32 [8, 4096], P('dp', 'seq'), may hold values from 0 to 1, as said below
- cotangent: bfloat16 [8, 4096, 768], P('dp', 'seq'), may hold values from -6 to 6
- in_weight: float32 [768, 3352], P(None, 'dp'), may hold values from -0.21875 to 0.21875
- out_weight: float32 [1536, 768], P('dp'), may hold values from -0.15625 to 0.15625
- vectors: float32 [11336], P('dp'), may hold values from -7 to 2.1
- in_moment: float32 [768, 3352], P(None, 'dp'), may hold values from -320 to 320
- out_moment: float32 [1536, 768], P('dp'), may hold values from -1024 to 1024
- vec_moment1: float32 [11336], P('dp'), may hold values from -32 to 32
- vec_moment2: float32 [11336], P('dp'), may hold values from 154.0096 to 622.592
Outputs:
- block_out: bfloat16 [8, 4096, 768], P('dp', 'seq')
- input_grad: float32 [8, 4096, 768], P('dp', 'seq')
- new_in_moment: float32 [768, 3352], P(None, 'dp')
- new_in_weight: float32 [768, 3352], P(None, 'dp')
- new_out_moment: float32 [1536, 768], P('dp')
- new_out_weight: float32 [1536, 768], P('dp')
- new_vec_moment1: float32 [11336], P('dp')
- new_vec_moment2: float32 [11336], P('dp')
- new_vectors: float32 [11336], P('dp')
The draws below stay inside these ranges and needn't reach their ends.
Inputs may be any that keep to these rules, and one draw needn't show every extreme that they name: No document starts at position 0 of a packed sequence or in the last 3 positions of any device's block of 512 positions; on each index of dp one of its 2 packed sequences has no start.
All inputs are finite; a program needn't handle non-finite values.
Results may differ from the reference program's by a relative error of at most 0.015.
The reference program's roundings to bfloat16 on the way count: a program that leaves them out, or rounds other values in their place, can miss the bound.
Values may be sent and summed in bfloat16 or wider, within the bound.
A program may use at most 512 MiB of HBM per device.

```python
import math
from functools import partial
import jax
import jax.numpy as jnp
from jax import lax

D = 768
H = 24
P_SIZE = 64
N = 128
E = 1536
CONV = 1792
IN = 3352
KW = 4
V = 11336
BLOCK = 256
LOC = 512
SEQS = 2
ITERS = 5
STEP = 10
L = 4096
PACKS = 8
TOKENS_ALL = 32768
N_DP = 4


def draw_starts(key, part):
    key = jax.random.fold_in(key, 11)
    subkeys = jax.random.split(key, 3)
    position = jnp.arange(L)
    inner = position % LOC
    hits = jax.random.randint(subkeys[0], (PACKS, L), 0, 2 * LOC) == 0
    allowed = (inner < LOC - (KW - 1)) & (position > 0)
    forced_at = LOC + jax.random.randint(subkeys[1], (PACKS, 1), 0, LOC - (KW - 1))
    forced = position[None, :] == forced_at
    spanning_pick = jax.random.randint(subkeys[2], (N_DP, 1), 0, SEQS)
    spanning = (jnp.arange(PACKS) % SEQS)[:, None] == jnp.repeat(spanning_pick, SEQS, axis=0)
    flags = (hits & allowed[None, :] | forced) & jnp.logical_not(spanning)
    return flags.astype(jnp.int32)


def draw_vectors(key, part):
    key = jax.random.fold_in(key, 23)
    subkeys = jax.random.split(key, 7)
    gain_in = jax.random.uniform(subkeys[0], (D,), jnp.float32, 0.7, 1.3)
    gain_out = jax.random.uniform(subkeys[1], (E,), jnp.float32, 0.7, 1.3)
    conv_bias = jax.random.uniform(subkeys[2], (CONV,), jnp.float32, -0.5, 0.5)
    conv_taps = jax.random.uniform(subkeys[3], (KW * CONV,), jnp.float32, -0.5, 0.5)
    step_bias = jax.random.uniform(subkeys[4], (H,), jnp.float32, -7.0, -3.0)
    decay_log = jax.random.uniform(subkeys[5], (H,), jnp.float32, math.log(0.01), math.log(8.0))
    skip_gain = jax.random.uniform(subkeys[6], (H,), jnp.float32, 0.5, 1.5)
    return jnp.concatenate([gain_in, gain_out, conv_bias, conv_taps, step_bias, decay_log, skip_gain])


def block_scale(stream_key, shape, cuts, smallest, high):
    def one(dim, blocks):
        draws = jax.random.uniform(jax.random.fold_in(jax.random.fold_in(stream_key, 6), dim), (blocks,), jnp.float32, smallest / len(cuts), high / len(cuts))
        return jnp.repeat(jnp.exp(draws), shape[dim] // blocks).reshape((-1,) + (1,) * (len(shape) - dim - 1))

    level = one(*cuts[0])
    for cut in cuts[1:]:
        level = level * one(*cut)
    return level


def bell_draw(rng, shape, scale, reach, cuts=(), kind=jnp.bfloat16):
    entries = jax.random.normal(rng, shape, jnp.float32) * scale
    if len(cuts) > 0:
        entries = block_scale(rng, shape, cuts, -0.22, 0.18) * entries
    return jnp.clip(entries, min=-reach, max=reach).astype(kind)


def setup_inputs(seed: int = 0) -> dict:
    arg_keys = jax.random.split(jax.random.key(seed), 11)
    tokens = bell_draw(arg_keys[0], (PACKS, L, D), 1.0, 6.0, ((0, 4), (1, 8)))
    starts = draw_starts(jax.random.fold_in(arg_keys[10], 71), 0)
    cotangent = bell_draw(arg_keys[2], (PACKS, L, D), 1.0, 6.0, ((0, 4), (1, 8)))
    in_weight = bell_draw(arg_keys[3], (D, IN), D ** -0.5, 0.21875, ((1, 4),), jnp.float32)
    out_weight = bell_draw(arg_keys[4], (E, D), E ** -0.5, 0.15625, ((0, 4),), jnp.float32)
    vectors = draw_vectors(jax.random.fold_in(arg_keys[10], 71), 0)
    in_moment = bell_draw(arg_keys[6], (D, IN), (0.3 * TOKENS_ALL ** 0.5), 320.0, ((1, 4),), jnp.float32)
    out_moment = bell_draw(arg_keys[7], (E, D), (TOKENS_ALL ** 0.5), 1024.0, ((0, 4),), jnp.float32)
    vec_moment1 = bell_draw(arg_keys[8], (V,), (0.033 * TOKENS_ALL ** 0.5), 32.0, ((0, 4),), jnp.float32)
    vec_moment2 = jnp.clip(jnp.exp(math.log(622.592) - 1.3968765 * jax.random.uniform(arg_keys[9], (V,), jnp.float32) ** block_scale(arg_keys[9], (V,), ((0, 4),), -0.2, 0.2)), 154.0096, 622.592)
    return {"tokens": tokens, "starts": starts, "cotangent": cotangent, "in_weight": in_weight, "out_weight": out_weight, "vectors": vectors, "in_moment": in_moment, "out_moment": out_moment, "vec_moment1": vec_moment1, "vec_moment2": vec_moment2}


EPSILON = 1e-05
MOMENTUM = 0.95
NS_A = 3.4445
NS_B = -4.775
NS_C = 2.0315
RATE_MATRIX = 0.5
RATE_VECTOR = 0.2
WEIGHT_DECAY = 0.01
BETA_FIRST = 0.9
BETA_SECOND = 0.95
ADAM_EPSILON = 1e-08
PRECISE = lax.Precision.HIGHEST

@jax.custom_vjp
def low(v):
    return lax.optimization_barrier(v.astype(jnp.bfloat16)).astype(jnp.float32)

@jax.custom_vjp
def low_back(v):
    return v

def low_keep(v):
    return (low(v), None)

def low_pass(kept, grad):
    return (grad,)

def back_keep(v):
    return (v, None)

def back_low(kept, grad):
    return (low(grad),)
low.defvjp(low_keep, low_pass)
low_back.defvjp(back_keep, back_low)

def split_vector(packed):
    offset = D + E + CONV
    gain_in = packed[:D]
    gain_out = packed[D:D + E]
    conv_bias = packed[D + E:offset]
    conv_taps = packed[offset:offset + KW * CONV].reshape(KW, CONV)
    offset = offset + KW * CONV
    step_bias = packed[offset:offset + H]
    decay_log = packed[offset + H:offset + 2 * H]
    skip_gain = packed[offset + 2 * H:offset + 3 * H]
    return (gain_in, gain_out, conv_bias, conv_taps, step_bias, decay_log, skip_gain)

def one_pack(inputs, starts, w_in, w_out, params):
    gain_in, gain_out, conv_bias, conv_taps, step_bias, decay_log, skip_gain = params
    seq_len = inputs.shape[0]
    inv_rms = lax.rsqrt(lax.optimization_barrier(jnp.mean(inputs * inputs, -1, keepdims=True)) + EPSILON)
    normed = low(inputs * inv_rms * gain_in)
    projected = low_back(jnp.dot(normed, w_in, precision=PRECISE))
    gate_pre = projected[:, :E]
    conv_input = low(projected[:, E:E + CONV])
    step_raw = projected[:, E + CONV:]
    doc_count = jnp.cumsum(starts)
    extended = jnp.concatenate([jnp.zeros((KW - 1, CONV), jnp.float32), conv_input], axis=0)
    count_ext = jnp.concatenate([jnp.full((KW - 1,), -1, doc_count.dtype), doc_count])
    conv_pre = conv_bias
    for tap_index in range(KW):
        tap_keep = (count_ext[tap_index:tap_index + seq_len] == doc_count).astype(jnp.float32)[:, None]
        conv_pre = conv_pre + extended[tap_index:tap_index + seq_len] * conv_taps[tap_index] * tap_keep
    activated = jax.nn.silu(conv_pre)
    x_part = activated[:, :E]
    b_part = activated[:, E:E + N]
    c_part = activated[:, E + N:]
    step_size = jax.nn.softplus(step_raw + step_bias)
    decay_rate = -jnp.exp(decay_log)
    log_decay = step_size * decay_rate
    count_blocks = seq_len // BLOCK
    pieces = (x_part.reshape(count_blocks, BLOCK, H, P_SIZE), b_part.reshape(count_blocks, BLOCK, N), c_part.reshape(count_blocks, BLOCK, N), step_size.reshape(count_blocks, BLOCK, H), log_decay.reshape(count_blocks, BLOCK, H), starts.reshape(count_blocks, BLOCK))
    lower = jnp.arange(BLOCK)[:, None] >= jnp.arange(BLOCK)[None, :]

    def block_step(state, piece):
        x_block, b_block, c_block, step_block, decay_block, start_block = piece
        x_low = low(x_block)
        b_low = low(b_block)
        c_low = low(c_block)
        cum_decay = jnp.cumsum(decay_block, axis=0)
        segment = jnp.cumsum(start_block)
        scores = low_back(jnp.dot(c_low, b_low.T, precision=PRECISE))
        pair_mask = (segment[:, None] == segment[None, :]) & lower
        cum_heads = cum_decay.T
        pair_gap = cum_heads[:, :, None] - cum_heads[:, None, :]
        pair_decay = jnp.exp(jnp.where(pair_mask[None], pair_gap, -jnp.inf))
        mix = low(scores[None] * pair_decay * step_block.T[:, None, :])
        y_diag = low_back(jnp.einsum('hts,shp->thp', mix, x_low, precision=PRECISE))
        end_same = (segment == segment[-1]).astype(jnp.float32)[:, None]
        end_decay = jnp.exp(cum_decay[-1] - cum_decay) * end_same
        x_weighted = low(x_low * (end_decay * step_block)[:, :, None])
        block_state = low_back(jnp.einsum('shp,sn->hpn', x_weighted, b_low, precision=PRECISE))
        block_decay = jnp.exp(cum_decay[-1]) * (segment[-1] == 0).astype(jnp.float32)
        y_carry = low_back(jnp.einsum('tn,hpn->thp', c_low, low(state), precision=PRECISE))
        carry_scale = jnp.exp(cum_decay) * (segment == 0).astype(jnp.float32)[:, None]
        y_block = y_diag + carry_scale[:, :, None] * y_carry + skip_gain[:, None] * x_block
        return (block_decay[:, None, None] * state + block_state, y_block.reshape(BLOCK, E))
    final_state, y_blocks = lax.scan(jax.checkpoint(block_step), jnp.zeros((H, P_SIZE, N), jnp.float32), pieces)
    mixed = y_blocks.reshape(seq_len, E)
    gated = mixed * jax.nn.silu(gate_pre)
    inv_gate = lax.rsqrt(lax.optimization_barrier(jnp.mean(gated * gated, -1, keepdims=True)) + EPSILON)
    gated_low = low(gated * inv_gate * gain_out)
    branch = low_back(jnp.dot(gated_low, w_out, precision=PRECISE))
    return inputs + branch

def forward(inputs, in_weight, out_weight, vectors, starts):
    w_in = low(in_weight)
    w_out = low(out_weight)
    params = split_vector(low(vectors))

    def per_pack(piece):
        return one_pack(piece[0], piece[1], w_in, w_out, params)
    return lax.map(jax.checkpoint(per_pack), (inputs, starts))

def orthogonalize(matrix):
    current = matrix / (jnp.sqrt(jnp.sum(matrix * matrix)) + 1e-07)
    for sweep_index in range(ITERS):
        gram = jnp.dot(current, current.T, precision=PRECISE)
        poly = NS_B * gram + NS_C * jnp.dot(gram, gram, precision=PRECISE)
        current = NS_A * current + jnp.dot(poly, current, precision=PRECISE)
    return current

def reference(tokens, starts, cotangent, in_weight, out_weight, vectors, in_moment, out_moment, vec_moment1, vec_moment2):
    inputs = tokens.astype(jnp.float32)
    outputs, pullback = jax.vjp(partial(forward, starts=starts), inputs, in_weight, out_weight, vectors)
    grad_inputs, grad_in, grad_out, grad_vec = pullback(cotangent.astype(jnp.float32))
    moment_in = MOMENTUM * in_moment + grad_in
    moment_out = MOMENTUM * out_moment + grad_out
    ortho_in = orthogonalize(moment_in)
    ortho_out = orthogonalize(moment_out.T).T
    weight_in = in_weight * (1.0 - RATE_MATRIX * WEIGHT_DECAY) - RATE_MATRIX * math.sqrt(IN / D) * ortho_in
    weight_out = out_weight * (1.0 - RATE_MATRIX * WEIGHT_DECAY) - RATE_MATRIX * math.sqrt(E / D) * ortho_out
    first = BETA_FIRST * vec_moment1 + (1.0 - BETA_FIRST) * grad_vec
    second = BETA_SECOND * vec_moment2 + (1.0 - BETA_SECOND) * grad_vec * grad_vec
    corrected = first / (1.0 - BETA_FIRST ** STEP) / (jnp.sqrt(second / (1.0 - BETA_SECOND ** STEP)) + ADAM_EPSILON)
    vec_new = vectors * (1.0 - RATE_VECTOR * WEIGHT_DECAY) - RATE_VECTOR * corrected
    return (outputs.astype(jnp.bfloat16), grad_inputs, moment_in, weight_in, moment_out, weight_out, first, second, vec_new)
```

```python
import jax
import jax.numpy as jnp
from jax import lax
from jax.sharding import PartitionSpec as P

D = 768
H = 24
P_SIZE = 64
N = 128
E = 1536
CONV = 1792
IN = 3352
KW = 4
BLOCK = 256
ITERS = 5
STEP = 10


EPSILON = 1e-05
MOMENTUM = 0.95
NS_A = 3.4445
NS_B = -4.775
NS_C = 2.0315
RATE_MATRIX = 0.5
RATE_VECTOR = 0.2
WEIGHT_DECAY = 0.01
BETA_FIRST = 0.9
BETA_SECOND = 0.95
ADAM_EPSILON = 1e-08
PRECISE = lax.Precision.HIGHEST


def from_behind(x, axis, by):
    devices = lax.axis_size(axis)
    pairs = [(i, i + by) for i in range(devices) if 0 <= i + by < devices]
    return lax.ppermute(x, axis, pairs)


def prefix(decay, state, axis, reverse):
    devices = lax.axis_size(axis)
    packs, heads, rows, cols = state.shape
    width = rows // devices * cols
    parts = state.reshape(packs * heads, devices, width)
    scales = jnp.broadcast_to(decay.reshape(packs * heads, 1, 1), (packs * heads, devices, cols))
    sent = jnp.moveaxis(jnp.concatenate([parts, scales], axis=2).astype(jnp.bfloat16), 1, 0)
    got = lax.all_to_all(sent, axis, 0, 0, tiled=True).astype(jnp.float32)
    before = jnp.zeros((packs * heads, width), jnp.float32)
    entering = [None] * devices
    for k in range(devices):
        at = devices - 1 - k if reverse else k
        entering[at] = before.astype(jnp.bfloat16)
        before = got[at, :, width : width + 1] * before + got[at, :, :width]
    back = lax.all_to_all(jnp.stack(entering), axis, 0, 0, tiled=True)
    return jnp.moveaxis(back, 0, 1).reshape(state.shape).astype(jnp.float32)


def orthogonal_factor(gram):
    size = gram.shape[0]
    eye = jnp.eye(size, dtype=jnp.float32)
    norm = jnp.sqrt(jnp.sum(gram * eye)) + 1e-07
    inverse = 1.0 / norm
    gram = gram * inverse * inverse
    factor = None
    for sweep_index in range(ITERS):
        precision = PRECISE if sweep_index < 2 else lax.Precision.HIGH
        square = jnp.dot(gram, gram, precision=precision)
        poly = NS_A * eye + NS_B * gram + NS_C * square
        factor = poly if factor is None else jnp.dot(poly, factor, precision=precision)
        if sweep_index < ITERS - 1:
            gram = jnp.dot(jnp.dot(poly, gram, precision=precision), poly, precision=precision)
    return factor * inverse


def split_vector(packed):
    offset = D + E + CONV
    gain_in = packed[:D]
    gain_out = packed[D : D + E]
    conv_bias = packed[D + E : offset]
    conv_taps = packed[offset : offset + KW * CONV].reshape(KW, CONV)
    offset = offset + KW * CONV
    step_bias = packed[offset : offset + H]
    decay_log = packed[offset + H : offset + 2 * H]
    skip_gain = packed[offset + 2 * H : offset + 3 * H]
    return (gain_in, gain_out, conv_bias, conv_taps, step_bias, decay_log, skip_gain)


def silu_slope(value):
    sigma = jax.nn.sigmoid(value)
    return sigma * (1.0 + value * (1.0 - sigma))


def per_device(
    tokens,
    starts,
    cotangent,
    in_weight,
    out_weight,
    vectors,
    in_moment,
    out_moment,
    vec_moment1,
    vec_moment2,
):
    w_in_low, w_out_low, vec_low = (
        lax.all_gather(in_weight.astype(jnp.bfloat16), "dp", axis=1, tiled=True),
        lax.all_gather(out_weight.astype(jnp.bfloat16), "dp", axis=0, tiled=True),
        lax.all_gather(vectors.astype(jnp.bfloat16), "dp", axis=0, tiled=True),
    )
    gain_in, gain_out, conv_bias, conv_taps, step_bias, decay_log, skip_gain = split_vector(
        vec_low.astype(jnp.float32)
    )
    pack_count = tokens.shape[0]
    local_rows = tokens.shape[1]
    block_count = local_rows // BLOCK
    edge_rows = KW - 1
    shape_blocks = (pack_count, block_count, BLOCK)
    inputs = tokens.astype(jnp.float32)
    inv_rms = lax.rsqrt(jnp.mean(inputs * inputs, -1, keepdims=True) + EPSILON)
    scaled = inputs * inv_rms
    normed = (scaled * gain_in).astype(jnp.bfloat16)
    projected = jnp.dot(normed, w_in_low, preferred_element_type=jnp.float32)
    gate_pre = projected[..., :E]
    conv_input = projected[..., E : E + CONV].astype(jnp.bfloat16)
    step_raw = projected[..., E + CONV :]
    edge = from_behind(conv_input[:, local_rows - edge_rows :, :], "seq", 1)
    extended = jnp.concatenate([edge, conv_input], axis=1).astype(jnp.float32)
    doc_count = jnp.cumsum(starts, axis=1)
    count_ext = jnp.concatenate(
        [jnp.zeros((pack_count, edge_rows), doc_count.dtype), doc_count], axis=1
    )
    tap_keep = [
        (count_ext[:, tap_index : tap_index + local_rows] == doc_count).astype(jnp.float32)[
            ..., None
        ]
        for tap_index in range(KW)
    ]
    conv_pre = conv_bias + extended[:, 0:local_rows] * conv_taps[0] * tap_keep[0]
    for tap_index in range(1, KW):
        conv_pre = (
            conv_pre
            + extended[:, tap_index : tap_index + local_rows]
            * conv_taps[tap_index]
            * tap_keep[tap_index]
        )
    activated = jax.nn.silu(conv_pre)
    step_arg = step_raw + step_bias
    step_size = jax.nn.softplus(step_arg)
    decay_rate = -jnp.exp(decay_log)
    log_decay = step_size * decay_rate
    x_full = activated[..., :E].reshape(shape_blocks + (H, P_SIZE))
    x_low = x_full.astype(jnp.bfloat16)
    b_low = activated[..., E : E + N].reshape(shape_blocks + (N,)).astype(jnp.bfloat16)
    c_low = activated[..., E + N :].reshape(shape_blocks + (N,)).astype(jnp.bfloat16)
    step_blocks = step_size.reshape(shape_blocks + (H,))
    cum_decay = jnp.cumsum(log_decay.reshape(shape_blocks + (H,)), axis=2)
    segment = jnp.cumsum(starts.reshape(shape_blocks), axis=2)
    lower = jnp.arange(BLOCK)[:, None] >= jnp.arange(BLOCK)[None, :]
    pair_mask = (segment[..., :, None] == segment[..., None, :]) & lower
    scores = jnp.einsum("abtn,absn->abts", c_low, b_low, preferred_element_type=jnp.float32)
    cum_heads = jnp.moveaxis(cum_decay, -1, 2)
    pair_gap = cum_heads[..., :, None] - cum_heads[..., None, :]
    pair_decay = jnp.exp(jnp.where(pair_mask[:, :, None], pair_gap, -jnp.inf))
    step_cols = jnp.moveaxis(step_blocks, -1, 2)[..., None, :]
    mix_full = scores[:, :, None] * pair_decay * step_cols
    mix_low = mix_full.astype(jnp.bfloat16)
    y_diag = jnp.einsum("abhts,abshp->abthp", mix_low, x_low, preferred_element_type=jnp.float32)
    end_same = (segment == segment[:, :, -1:]).astype(jnp.float32)[..., None]
    end_decay = jnp.exp(cum_decay[:, :, -1:, :] - cum_decay) * end_same
    end_weight = end_decay * step_blocks
    x_weighted = (x_low.astype(jnp.float32) * end_weight[..., None]).astype(jnp.bfloat16)
    block_state = jnp.einsum(
        "abshp,absn->abhpn", x_weighted, b_low, preferred_element_type=jnp.float32
    )
    block_decay = (
        jnp.exp(cum_decay[:, :, -1, :]) * (segment[:, :, -1] == 0).astype(jnp.float32)[..., None]
    )
    decay_total = block_decay[:, 0]
    state_total = block_state[:, 0]
    block_index = 1
    state_total = (
        block_decay[:, block_index][..., None, None] * state_total + block_state[:, block_index]
    )
    decay_total = decay_total * block_decay[:, block_index]
    entering = prefix(decay_total, state_total, "seq", False)
    state_list = [entering]
    block_index = 0
    state_list.append(
        block_decay[:, block_index][..., None, None] * state_list[-1] + block_state[:, block_index]
    )
    state_in = jnp.stack(state_list, axis=1)
    state_low = state_in.astype(jnp.bfloat16)
    y_carry = jnp.einsum("abtn,abhpn->abthp", c_low, state_low, preferred_element_type=jnp.float32)
    carry_scale = jnp.exp(cum_decay) * (segment == 0).astype(jnp.float32)[..., None]
    y_blocks = y_diag + carry_scale[..., None] * y_carry + skip_gain[:, None] * x_full
    mixed = y_blocks.reshape(pack_count, local_rows, E)
    gate_act = jax.nn.silu(gate_pre)
    gated = mixed * gate_act
    inv_gate = lax.rsqrt(jnp.mean(gated * gated, -1, keepdims=True) + EPSILON)
    gated_hat = gated * inv_gate
    gated_low = (gated_hat * gain_out).astype(jnp.bfloat16)
    branch = jnp.dot(gated_low, w_out_low, preferred_element_type=jnp.float32)
    result = (inputs + branch).astype(jnp.bfloat16)
    grad_w_out = jnp.einsum("ate,atd->ed", gated_low, cotangent, preferred_element_type=jnp.float32)
    grad_ghat = jnp.einsum("atd,ed->ate", cotangent, w_out_low, preferred_element_type=jnp.float32)
    grad_gain_out = jnp.sum(grad_ghat * gated_hat, axis=(0, 1))
    grad_scaled_gate = grad_ghat * gain_out
    grad_gated = inv_gate * (
        grad_scaled_gate - gated_hat * jnp.mean(grad_scaled_gate * gated_hat, -1, keepdims=True)
    )
    grad_mixed = grad_gated * gate_act
    grad_gate = grad_gated * mixed * silu_slope(gate_pre)
    grad_y = grad_mixed.reshape(shape_blocks + (H, P_SIZE))
    grad_diag_low = grad_y.astype(jnp.bfloat16)
    grad_carry_low = (carry_scale[..., None] * grad_y).astype(jnp.bfloat16)
    grad_cum = jnp.sum(grad_y * y_carry, -1) * carry_scale
    grad_skip = jnp.sum(grad_y * x_full, axis=(0, 1, 2, 4))
    grad_x = skip_gain[:, None] * grad_y
    grad_mix = jnp.einsum(
        "abthp,abshp->abhts", grad_diag_low, x_low, preferred_element_type=jnp.float32
    )
    grad_x = grad_x + jnp.einsum(
        "abhts,abthp->abshp", mix_low, grad_diag_low, preferred_element_type=jnp.float32
    )
    grad_c = jnp.einsum(
        "abthp,abhpn->abtn", grad_carry_low, state_low, preferred_element_type=jnp.float32
    )
    grad_state_in = jnp.einsum(
        "abthp,abtn->abhpn", grad_carry_low, c_low, preferred_element_type=jnp.float32
    )
    local_adjoint = grad_state_in[:, block_count - 1]
    block_index = 0
    local_adjoint = (
        grad_state_in[:, block_index] + block_decay[:, block_index][..., None, None] * local_adjoint
    )
    adjoint_next = prefix(decay_total, local_adjoint, "seq", True)
    state_grads = [None] * block_count
    decay_grads = [None] * block_count
    for block_index in range(block_count - 1, -1, -1):
        state_grads[block_index] = adjoint_next
        decay_grads[block_index] = jnp.sum(adjoint_next * state_in[:, block_index], axis=(-2, -1))
        adjoint_next = (
            grad_state_in[:, block_index]
            + block_decay[:, block_index][..., None, None] * adjoint_next
        )
    grad_state_low = jnp.stack(state_grads, axis=1).astype(jnp.bfloat16)
    grad_block_decay = jnp.stack(decay_grads, axis=1)
    grad_xw = jnp.einsum(
        "abhpn,absn->abshp", grad_state_low, b_low, preferred_element_type=jnp.float32
    )
    grad_b = jnp.einsum(
        "abhpn,abshp->absn", grad_state_low, x_weighted, preferred_element_type=jnp.float32
    )
    grad_x = grad_x + grad_xw * end_weight[..., None]
    grad_end = jnp.sum(grad_xw * x_low.astype(jnp.float32), -1)
    grad_step = grad_end * end_decay
    grad_gap = grad_end * end_weight
    grad_cum = grad_cum - grad_gap
    last_extra = jnp.sum(grad_gap, axis=2) + grad_block_decay * block_decay
    grad_cum = jnp.concatenate(
        [grad_cum[:, :, :-1], grad_cum[:, :, -1:] + last_extra[:, :, None]], axis=2
    )
    product = grad_mix * mix_full
    grad_cum = grad_cum + jnp.moveaxis(jnp.sum(product, -1) - jnp.sum(product, -2), 2, 3)
    grad_step = grad_step + jnp.moveaxis(
        jnp.sum(grad_mix * scores[:, :, None] * pair_decay, axis=3), 2, 3
    )
    grad_scores = jnp.sum(grad_mix * pair_decay * step_cols, axis=2).astype(jnp.bfloat16)
    grad_c = grad_c + jnp.einsum(
        "abts,absn->abtn", grad_scores, b_low, preferred_element_type=jnp.float32
    )
    grad_b = grad_b + jnp.einsum(
        "abts,abtn->absn", grad_scores, c_low, preferred_element_type=jnp.float32
    )
    grad_log = jnp.flip(jnp.cumsum(jnp.flip(grad_cum, 2), axis=2), 2)
    grad_step = grad_step + grad_log * decay_rate
    grad_decay_log = jnp.sum(grad_log * step_blocks, axis=(0, 1, 2)) * decay_rate
    grad_arg = grad_step.reshape(pack_count, local_rows, H) * jax.nn.sigmoid(step_arg)
    grad_step_bias = jnp.sum(grad_arg, axis=(0, 1))
    grad_act = jnp.concatenate(
        [
            grad_x.reshape(pack_count, local_rows, E),
            grad_b.reshape(pack_count, local_rows, N),
            grad_c.reshape(pack_count, local_rows, N),
        ],
        axis=-1,
    )
    grad_pre = grad_act * silu_slope(conv_pre)
    grad_conv_bias = jnp.sum(grad_pre, axis=(0, 1))
    grad_taps = jnp.stack(
        [
            jnp.sum(
                grad_pre * extended[:, tap_index : tap_index + local_rows] * tap_keep[tap_index],
                axis=(0, 1),
            )
            for tap_index in range(KW)
        ]
    )
    grad_ext = jnp.zeros((pack_count, local_rows + edge_rows, CONV), jnp.float32)
    for tap_index in range(KW):
        grad_ext = grad_ext + jnp.pad(
            grad_pre * conv_taps[tap_index] * tap_keep[tap_index],
            ((0, 0), (tap_index, edge_rows - tap_index), (0, 0)),
        )
    grad_edge = from_behind(grad_ext[:, :edge_rows].astype(jnp.bfloat16), "seq", -1).astype(
        jnp.float32
    )
    grad_conv_in = jnp.concatenate(
        [grad_ext[:, edge_rows:local_rows], grad_ext[:, local_rows:] + grad_edge], axis=1
    )
    grad_projected = jnp.concatenate([grad_gate, grad_conv_in, grad_arg], axis=-1).astype(
        jnp.bfloat16
    )
    owners = lax.axis_size("dp")
    owner_out = lax.psum(
        lax.psum_scatter(grad_w_out, "dp", scatter_dimension=0, tiled=True), "seq"
    )
    grad_projected, owner_out = lax.optimization_barrier((grad_projected, owner_out))
    grad_w_in = jnp.einsum(
        "atj,atd->jd", grad_projected, normed, preferred_element_type=jnp.float32
    ).astype(jnp.bfloat16)
    owner_in = lax.psum(
        lax.psum_scatter(
            grad_w_in.reshape(owners, IN // owners, D), "dp", scatter_dimension=0, tiled=False
        ),
        "seq",
    )
    owner_in = owner_in.astype(jnp.float32).T
    grad_normed = jnp.einsum(
        "atj,dj->atd", grad_projected, w_in_low, preferred_element_type=jnp.float32
    )
    grad_gain_in = jnp.sum(grad_normed * scaled, axis=(0, 1))
    grad_scaled = grad_normed * gain_in
    grad_inputs = inv_rms * (
        grad_scaled - scaled * jnp.mean(grad_scaled * scaled, -1, keepdims=True)
    ) + cotangent.astype(jnp.float32)
    grad_vec = jnp.concatenate(
        [
            grad_gain_in,
            grad_gain_out,
            grad_conv_bias,
            grad_taps.reshape(-1),
            grad_step_bias,
            grad_decay_log,
            grad_skip,
        ]
    )
    summed_vec = lax.psum(grad_vec, ("seq", "dp"))
    vec_rows = vectors.shape[0]
    owner_vec = lax.dynamic_slice(summed_vec, (lax.axis_index("dp") * vec_rows,), (vec_rows,))
    moment_out = MOMENTUM * out_moment + owner_out
    gram_out = lax.psum(jnp.dot(moment_out.T, moment_out, precision=PRECISE), "dp")
    moment_in = MOMENTUM * in_moment + owner_in
    gram_in = jnp.dot(moment_in, moment_in.T, precision=PRECISE)
    gram_in, gram_out = lax.optimization_barrier((gram_in, gram_out))
    gram_in = lax.psum(gram_in, "dp")
    factor_out = orthogonal_factor(gram_out)
    ortho_out = jnp.dot(moment_out, factor_out.T, precision=lax.Precision.HIGH)
    factor_in = orthogonal_factor(gram_in)
    ortho_in = jnp.dot(factor_in, moment_in, precision=lax.Precision.HIGH)
    weight_in = (
        in_weight * (1.0 - RATE_MATRIX * WEIGHT_DECAY) - RATE_MATRIX * (IN / D) ** 0.5 * ortho_in
    )
    weight_out = (
        out_weight * (1.0 - RATE_MATRIX * WEIGHT_DECAY) - RATE_MATRIX * (E / D) ** 0.5 * ortho_out
    )
    first = BETA_FIRST * vec_moment1 + (1.0 - BETA_FIRST) * owner_vec
    second = BETA_SECOND * vec_moment2 + (1.0 - BETA_SECOND) * owner_vec * owner_vec
    corrected = (
        first
        / (1.0 - BETA_FIRST**STEP)
        / (jnp.sqrt(second / (1.0 - BETA_SECOND**STEP)) + ADAM_EPSILON)
    )
    vec_new = vectors * (1.0 - RATE_VECTOR * WEIGHT_DECAY) - RATE_VECTOR * corrected
    return (
        result,
        grad_inputs,
        moment_in,
        weight_in,
        moment_out,
        weight_out,
        first,
        second,
        vec_new,
    )


def solution(mesh):
    placed = (
        P("dp", "seq", None),
        P("dp", "seq"),
        P("dp", "seq", None),
        P(None, "dp"),
        P("dp", None),
        P("dp"),
        P(None, "dp"),
        P("dp", None),
        P("dp"),
        P("dp"),
    )
    return jax.shard_map(
        per_device,
        mesh=mesh,
        in_specs=placed,
        out_specs=(
            P("dp", "seq", None),
            P("dp", "seq", None),
            P(None, "dp"),
            P(None, "dp"),
            P("dp", None),
            P("dp", None),
            P("dp"),
            P("dp"),
            P("dp"),
        ),
        check_vma=False,
    )
```

```python
import jax
import jax.numpy as jnp
from jax import lax
from jax.sharding import PartitionSpec as P

D = 768
H = 24
P_SIZE = 64
N = 128
E = 1536
CONV = 1792
IN = 3352
KW = 4
BLOCK = 256
ITERS = 5
STEP = 10


EPSILON = 1e-05
MOMENTUM = 0.95
NS_A = 3.4445
NS_B = -4.775
NS_C = 2.0315
RATE_MATRIX = 0.5
RATE_VECTOR = 0.2
WEIGHT_DECAY = 0.01
BETA_FIRST = 0.9
BETA_SECOND = 0.95
ADAM_EPSILON = 1e-08
PRECISE = lax.Precision.HIGHEST


def from_behind(x, axis, by):
    devices = lax.axis_size(axis)
    pairs = [(i, i + by) for i in range(devices) if 0 <= i + by < devices]
    return lax.ppermute(x, axis, pairs)


def prefix(decay, state, axis, reverse):
    devices = lax.axis_size(axis)
    packs, heads, rows, cols = state.shape
    width = rows // devices * cols
    parts = state.reshape(packs * heads, devices, width)
    scales = jnp.broadcast_to(decay.reshape(packs * heads, 1, 1), (packs * heads, devices, cols))
    sent = jnp.moveaxis(jnp.concatenate([parts, scales], axis=2).astype(jnp.bfloat16), 1, 0)
    got = lax.all_to_all(sent, axis, 0, 0, tiled=True).astype(jnp.float32)
    before = jnp.zeros((packs * heads, width), jnp.float32)
    entering = [None] * devices
    for k in range(devices):
        at = devices - 1 - k if reverse else k
        entering[at] = before.astype(jnp.bfloat16)
        before = got[at, :, width : width + 1] * before + got[at, :, :width]
    back = lax.all_to_all(jnp.stack(entering), axis, 0, 0, tiled=True)
    return jnp.moveaxis(back, 0, 1).reshape(state.shape).astype(jnp.float32)


def orthogonal_factor(gram):
    size = gram.shape[0]
    eye = jnp.eye(size, dtype=jnp.float32)
    norm = jnp.sqrt(jnp.sum(gram * eye)) + 1e-07
    inverse = 1.0 / norm
    gram = gram * inverse * inverse
    factor = None
    for sweep_index in range(ITERS):
        precision = PRECISE if sweep_index < 2 else lax.Precision.HIGH
        square = jnp.dot(gram, gram, precision=precision)
        poly = NS_A * eye + NS_B * gram + NS_C * square
        factor = poly if factor is None else jnp.dot(poly, factor, precision=precision)
        if sweep_index < ITERS - 1:
            gram = jnp.dot(jnp.dot(poly, gram, precision=precision), poly, precision=precision)
    return factor * inverse


def split_vector(packed):
    offset = D + E + CONV
    gain_in = packed[:D]
    gain_out = packed[D : D + E]
    conv_bias = packed[D + E : offset]
    conv_taps = packed[offset : offset + KW * CONV].reshape(KW, CONV)
    offset = offset + KW * CONV
    step_bias = packed[offset : offset + H]
    decay_log = packed[offset + H : offset + 2 * H]
    skip_gain = packed[offset + 2 * H : offset + 3 * H]
    return (gain_in, gain_out, conv_bias, conv_taps, step_bias, decay_log, skip_gain)


def silu_slope(value):
    sigma = jax.nn.sigmoid(value)
    return sigma * (1.0 + value * (1.0 - sigma))


def per_device(
    tokens,
    starts,
    cotangent,
    in_weight,
    out_weight,
    vectors,
    in_moment,
    out_moment,
    vec_moment1,
    vec_moment2,
):
    w_in_low, w_out_low, vec_low = (
        lax.all_gather(in_weight.astype(jnp.bfloat16), "dp", axis=1, tiled=True),
        lax.all_gather(out_weight.astype(jnp.bfloat16), "dp", axis=0, tiled=True),
        lax.all_gather(vectors.astype(jnp.bfloat16), "dp", axis=0, tiled=True),
    )
    gain_in, gain_out, conv_bias, conv_taps, step_bias, decay_log, skip_gain = split_vector(
        vec_low.astype(jnp.float32)
    )
    pack_count = tokens.shape[0]
    local_rows = tokens.shape[1]
    block_count = local_rows // BLOCK
    edge_rows = KW - 1
    shape_blocks = (pack_count, block_count, BLOCK)
    inputs = tokens.astype(jnp.float32)
    inv_rms = lax.rsqrt(jnp.mean(inputs * inputs, -1, keepdims=True) + EPSILON)
    scaled = inputs * inv_rms
    normed = (scaled * gain_in).astype(jnp.bfloat16)
    w_gate, w_conv, w_step = (
        w_in_low[:, :E],
        w_in_low[:, E : E + CONV],
        w_in_low[:, E + CONV :],
    )
    gate_pre = jnp.dot(normed, w_gate, preferred_element_type=jnp.float32)
    conv_input = jnp.dot(normed, w_conv, preferred_element_type=jnp.float32).astype(jnp.bfloat16)
    step_raw = jnp.dot(normed, w_step, preferred_element_type=jnp.float32)
    edge = from_behind(conv_input[:, local_rows - edge_rows :, :], "seq", 1)
    extended = jnp.concatenate([edge, conv_input], axis=1).astype(jnp.float32)
    doc_count = jnp.cumsum(starts, axis=1)
    count_ext = jnp.concatenate(
        [jnp.zeros((pack_count, edge_rows), doc_count.dtype), doc_count], axis=1
    )
    tap_keep = [
        (count_ext[:, tap_index : tap_index + local_rows] == doc_count).astype(jnp.float32)[
            ..., None
        ]
        for tap_index in range(KW)
    ]
    conv_pre = conv_bias + extended[:, 0:local_rows] * conv_taps[0] * tap_keep[0]
    for tap_index in range(1, KW):
        conv_pre = (
            conv_pre
            + extended[:, tap_index : tap_index + local_rows]
            * conv_taps[tap_index]
            * tap_keep[tap_index]
        )
    activated = jax.nn.silu(conv_pre)
    step_arg = step_raw + step_bias
    step_size = jax.nn.softplus(step_arg)
    decay_rate = -jnp.exp(decay_log)
    log_decay = step_size * decay_rate
    x_full = activated[..., :E].reshape(shape_blocks + (H, P_SIZE))
    x_low = x_full.astype(jnp.bfloat16)
    b_low = activated[..., E : E + N].reshape(shape_blocks + (N,)).astype(jnp.bfloat16)
    c_low = activated[..., E + N :].reshape(shape_blocks + (N,)).astype(jnp.bfloat16)
    step_blocks = step_size.reshape(shape_blocks + (H,))
    cum_decay = jnp.cumsum(log_decay.reshape(shape_blocks + (H,)), axis=2)
    segment = jnp.cumsum(starts.reshape(shape_blocks), axis=2)
    lower = jnp.arange(BLOCK)[:, None] >= jnp.arange(BLOCK)[None, :]
    pair_mask = (segment[..., :, None] == segment[..., None, :]) & lower
    scores = jnp.einsum("abtn,absn->abts", c_low, b_low, preferred_element_type=jnp.float32)
    cum_heads = jnp.moveaxis(cum_decay, -1, 2)
    pair_gap = cum_heads[..., :, None] - cum_heads[..., None, :]
    pair_decay = jnp.exp(jnp.where(pair_mask[:, :, None], pair_gap, -jnp.inf))
    step_cols = jnp.moveaxis(step_blocks, -1, 2)[..., None, :]
    mix_full = scores[:, :, None] * pair_decay * step_cols
    mix_low = mix_full.astype(jnp.bfloat16)
    y_diag = jnp.einsum("abhts,abshp->abthp", mix_low, x_low, preferred_element_type=jnp.float32)
    end_same = (segment == segment[:, :, -1:]).astype(jnp.float32)[..., None]
    end_decay = jnp.exp(cum_decay[:, :, -1:, :] - cum_decay) * end_same
    end_weight = end_decay * step_blocks
    x_weighted = (x_low.astype(jnp.float32) * end_weight[..., None]).astype(jnp.bfloat16)
    block_state = jnp.einsum(
        "abshp,absn->abhpn", x_weighted, b_low, preferred_element_type=jnp.float32
    )
    block_decay = (
        jnp.exp(cum_decay[:, :, -1, :]) * (segment[:, :, -1] == 0).astype(jnp.float32)[..., None]
    )
    decay_total = block_decay[:, 0]
    state_total = block_state[:, 0]
    block_index = 1
    state_total = (
        block_decay[:, block_index][..., None, None] * state_total + block_state[:, block_index]
    )
    decay_total = decay_total * block_decay[:, block_index]
    entering = prefix(decay_total, state_total, "seq", False)
    state_list = [entering]
    block_index = 0
    state_list.append(
        block_decay[:, block_index][..., None, None] * state_list[-1] + block_state[:, block_index]
    )
    state_in = jnp.stack(state_list, axis=1)
    state_low = state_in.astype(jnp.bfloat16)
    y_carry = jnp.einsum("abtn,abhpn->abthp", c_low, state_low, preferred_element_type=jnp.float32)
    carry_scale = jnp.exp(cum_decay) * (segment == 0).astype(jnp.float32)[..., None]
    y_blocks = y_diag + carry_scale[..., None] * y_carry + skip_gain[:, None] * x_full
    mixed = y_blocks.reshape(pack_count, local_rows, E)
    gate_act = jax.nn.silu(gate_pre)
    gated = mixed * gate_act
    inv_gate = lax.rsqrt(jnp.mean(gated * gated, -1, keepdims=True) + EPSILON)
    gated_hat = gated * inv_gate
    gated_low = (gated_hat * gain_out).astype(jnp.bfloat16)
    branch = jnp.dot(gated_low, w_out_low, preferred_element_type=jnp.float32)
    result = (inputs + branch).astype(jnp.bfloat16)
    grad_w_out = jnp.einsum("ate,atd->ed", gated_low, cotangent, preferred_element_type=jnp.float32)
    grad_ghat = jnp.einsum("atd,ed->ate", cotangent, w_out_low, preferred_element_type=jnp.float32)
    grad_w_out, grad_ghat = lax.optimization_barrier((grad_w_out, grad_ghat))
    owner_out = lax.psum(
        lax.psum_scatter(
            grad_w_out.astype(jnp.bfloat16), "dp", scatter_dimension=0, tiled=True
        ),
        "seq",
    ).astype(jnp.float32)
    moment_out = MOMENTUM * out_moment + owner_out
    gram_out = lax.psum(jnp.dot(moment_out.T, moment_out, precision=PRECISE), "dp")
    grad_gain_out = jnp.sum(grad_ghat * gated_hat, axis=(0, 1))
    grad_scaled_gate = grad_ghat * gain_out
    grad_gated = inv_gate * (
        grad_scaled_gate - gated_hat * jnp.mean(grad_scaled_gate * gated_hat, -1, keepdims=True)
    )
    grad_mixed = grad_gated * gate_act
    grad_gate = grad_gated * mixed * silu_slope(gate_pre)
    grad_y = grad_mixed.reshape(shape_blocks + (H, P_SIZE))
    grad_diag_low = grad_y.astype(jnp.bfloat16)
    grad_carry_low = (carry_scale[..., None] * grad_y).astype(jnp.bfloat16)
    grad_cum = jnp.sum(grad_y * y_carry, -1) * carry_scale
    grad_skip = jnp.sum(grad_y * x_full, axis=(0, 1, 2, 4))
    grad_x = skip_gain[:, None] * grad_y
    grad_mix = jnp.einsum(
        "abthp,abshp->abhts", grad_diag_low, x_low, preferred_element_type=jnp.float32
    )
    grad_x = grad_x + jnp.einsum(
        "abhts,abthp->abshp", mix_low, grad_diag_low, preferred_element_type=jnp.float32
    )
    grad_c = jnp.einsum(
        "abthp,abhpn->abtn", grad_carry_low, state_low, preferred_element_type=jnp.float32
    )
    grad_state_in = jnp.einsum(
        "abthp,abtn->abhpn", grad_carry_low, c_low, preferred_element_type=jnp.float32
    )
    local_adjoint = grad_state_in[:, block_count - 1]
    block_index = 0
    local_adjoint = (
        grad_state_in[:, block_index] + block_decay[:, block_index][..., None, None] * local_adjoint
    )
    adjoint_next = prefix(decay_total, local_adjoint, "seq", True)
    state_grads = [None] * block_count
    decay_grads = [None] * block_count
    for block_index in range(block_count - 1, -1, -1):
        state_grads[block_index] = adjoint_next
        decay_grads[block_index] = jnp.sum(adjoint_next * state_in[:, block_index], axis=(-2, -1))
        adjoint_next = (
            grad_state_in[:, block_index]
            + block_decay[:, block_index][..., None, None] * adjoint_next
        )
    grad_state_low = jnp.stack(state_grads, axis=1).astype(jnp.bfloat16)
    grad_block_decay = jnp.stack(decay_grads, axis=1)
    grad_xw = jnp.einsum(
        "abhpn,absn->abshp", grad_state_low, b_low, preferred_element_type=jnp.float32
    )
    grad_b = jnp.einsum(
        "abhpn,abshp->absn", grad_state_low, x_weighted, preferred_element_type=jnp.float32
    )
    grad_x = grad_x + grad_xw * end_weight[..., None]
    grad_end = jnp.sum(grad_xw * x_low.astype(jnp.float32), -1)
    grad_step = grad_end * end_decay
    grad_gap = grad_end * end_weight
    grad_cum = grad_cum - grad_gap
    last_extra = jnp.sum(grad_gap, axis=2) + grad_block_decay * block_decay
    grad_cum = jnp.concatenate(
        [grad_cum[:, :, :-1], grad_cum[:, :, -1:] + last_extra[:, :, None]], axis=2
    )
    product = grad_mix * mix_full
    grad_cum = grad_cum + jnp.moveaxis(jnp.sum(product, -1) - jnp.sum(product, -2), 2, 3)
    grad_step = grad_step + jnp.moveaxis(
        jnp.sum(grad_mix * scores[:, :, None] * pair_decay, axis=3), 2, 3
    )
    grad_scores = jnp.sum(grad_mix * pair_decay * step_cols, axis=2).astype(jnp.bfloat16)
    grad_c = grad_c + jnp.einsum(
        "abts,absn->abtn", grad_scores, b_low, preferred_element_type=jnp.float32
    )
    grad_b = grad_b + jnp.einsum(
        "abts,abtn->absn", grad_scores, c_low, preferred_element_type=jnp.float32
    )
    grad_log = jnp.flip(jnp.cumsum(jnp.flip(grad_cum, 2), axis=2), 2)
    grad_step = grad_step + grad_log * decay_rate
    grad_decay_log = jnp.sum(grad_log * step_blocks, axis=(0, 1, 2)) * decay_rate
    grad_arg = grad_step.reshape(pack_count, local_rows, H) * jax.nn.sigmoid(step_arg)
    grad_step_bias = jnp.sum(grad_arg, axis=(0, 1))
    grad_act = jnp.concatenate(
        [
            grad_x.reshape(pack_count, local_rows, E),
            grad_b.reshape(pack_count, local_rows, N),
            grad_c.reshape(pack_count, local_rows, N),
        ],
        axis=-1,
    )
    grad_pre = grad_act * silu_slope(conv_pre)
    grad_conv_bias = jnp.sum(grad_pre, axis=(0, 1))
    grad_taps = jnp.stack(
        [
            jnp.sum(
                grad_pre * extended[:, tap_index : tap_index + local_rows] * tap_keep[tap_index],
                axis=(0, 1),
            )
            for tap_index in range(KW)
        ]
    )
    grad_ext = jnp.zeros((pack_count, local_rows + edge_rows, CONV), jnp.float32)
    for tap_index in range(KW):
        grad_ext = grad_ext + jnp.pad(
            grad_pre * conv_taps[tap_index] * tap_keep[tap_index],
            ((0, 0), (tap_index, edge_rows - tap_index), (0, 0)),
        )
    grad_edge = from_behind(grad_ext[:, :edge_rows].astype(jnp.bfloat16), "seq", -1).astype(
        jnp.float32
    )
    grad_conv_in = jnp.concatenate(
        [grad_ext[:, edge_rows:local_rows], grad_ext[:, local_rows:] + grad_edge], axis=1
    )
    grad_conv_in, gram_out = lax.optimization_barrier(
        (grad_conv_in.astype(jnp.bfloat16), gram_out)
    )
    grad_parts = (grad_gate.astype(jnp.bfloat16), grad_conv_in, grad_arg.astype(jnp.bfloat16))
    owners = lax.axis_size("dp")
    grad_w_in = jnp.concatenate(
        [
            jnp.einsum("atj,atd->jd", part, normed, preferred_element_type=jnp.float32).astype(
                jnp.bfloat16
            )
            for part in grad_parts
        ],
        axis=0,
    )
    owner_in = lax.psum(
        lax.psum_scatter(
            grad_w_in.reshape(owners, IN // owners, D), "dp", scatter_dimension=0, tiled=False
        ),
        "seq",
    )
    owner_in = owner_in.astype(jnp.float32).T
    grad_normed = sum(
        jnp.einsum("atj,dj->atd", part, weight, preferred_element_type=jnp.float32)
        for part, weight in zip(grad_parts, (w_gate, w_conv, w_step))
    )
    grad_gain_in = jnp.sum(grad_normed * scaled, axis=(0, 1))
    grad_scaled = grad_normed * gain_in
    grad_inputs = inv_rms * (
        grad_scaled - scaled * jnp.mean(grad_scaled * scaled, -1, keepdims=True)
    ) + cotangent.astype(jnp.float32)
    grad_vec = jnp.concatenate(
        [
            grad_gain_in,
            grad_gain_out,
            grad_conv_bias,
            grad_taps.reshape(-1),
            grad_step_bias,
            grad_decay_log,
            grad_skip,
        ]
    )
    summed_vec = lax.psum(grad_vec, ("seq", "dp"))
    vec_rows = vectors.shape[0]
    owner_vec = lax.dynamic_slice(summed_vec, (lax.axis_index("dp") * vec_rows,), (vec_rows,))
    moment_in = MOMENTUM * in_moment + owner_in
    gram_in = lax.psum(jnp.dot(moment_in, moment_in.T, precision=PRECISE), "dp")
    factor_out = orthogonal_factor(gram_out)
    ortho_out = jnp.dot(moment_out, factor_out.T, precision=lax.Precision.HIGH)
    factor_in = orthogonal_factor(gram_in)
    ortho_in = jnp.dot(factor_in, moment_in, precision=lax.Precision.HIGH)
    weight_in = (
        in_weight * (1.0 - RATE_MATRIX * WEIGHT_DECAY) - RATE_MATRIX * (IN / D) ** 0.5 * ortho_in
    )
    weight_out = (
        out_weight * (1.0 - RATE_MATRIX * WEIGHT_DECAY) - RATE_MATRIX * (E / D) ** 0.5 * ortho_out
    )
    first = BETA_FIRST * vec_moment1 + (1.0 - BETA_FIRST) * owner_vec
    second = BETA_SECOND * vec_moment2 + (1.0 - BETA_SECOND) * owner_vec * owner_vec
    corrected = (
        first
        / (1.0 - BETA_FIRST**STEP)
        / (jnp.sqrt(second / (1.0 - BETA_SECOND**STEP)) + ADAM_EPSILON)
    )
    vec_new = vectors * (1.0 - RATE_VECTOR * WEIGHT_DECAY) - RATE_VECTOR * corrected
    return (
        result,
        grad_inputs,
        moment_in,
        weight_in,
        moment_out,
        weight_out,
        first,
        second,
        vec_new,
    )


def solution(mesh):
    placed = (
        P("dp", "seq", None),
        P("dp", "seq"),
        P("dp", "seq", None),
        P(None, "dp"),
        P("dp", None),
        P("dp"),
        P(None, "dp"),
        P("dp", None),
        P("dp"),
        P("dp"),
    )
    return jax.shard_map(
        per_device,
        mesh=mesh,
        in_specs=placed,
        out_specs=(
            P("dp", "seq", None),
            P("dp", "seq", None),
            P(None, "dp"),
            P(None, "dp"),
            P("dp", None),
            P("dp", None),
            P("dp"),
            P("dp"),
            P("dp"),
        ),
        check_vma=False,
    )
```
